32 devices in a mesh: oi: 4 (over z), oj: 8 (over y, x, core).
Axes of the slice: x: 2, y: 2, z: 4, core: 2. Of those that a mesh axis runs over, the one named last changes fastest.
Arguments:
- amplitudes: bfloat16 [768, 128, 128], P(('oi', 'oj')), may hold values from -6 to 6
- exchange_ints: bfloat16 [768, 128, 128], P(('oi', 'oj')), may hold values from -6 to 6
- row_intersection: bfloat16 [768, 128, 128], P(('oi', 'oj')), may hold values from -0.5 to 0.5
- col_intersection: bfloat16 [768, 128, 128], P(('oi', 'oj')), may hold values from -0.5 to 0.5
- pno_energy: float32 [768, 128], P(('oi', 'oj')), may hold values from 0.2 to 1
- row_fock: float32 [768], P(('oi', 'oj')), may hold values from -1 to 1
- col_fock: float32 [768], P(('oi', 'oj')), may hold values from -1 to 1
- pair_occ: int32 [768, 2], P(('oi', 'oj')), may hold values from 0 to 19999
- fock_occ: float32 [20000], replicated, may hold values from -0.6 to -0.2
- row_peer: int32 [768, 1], P(('oi', 'oj')), may hold values from 0 to 7; in each aligned block of 24 rows (0 to 23, 24 to 47, ...) at most 4 rows name the same one
- row_slot: int32 [768], P(('oi', 'oj')), may hold values from 0 to 23
- col_peer: int32 [768, 1], P(('oi', 'oj')), may hold values from 0 to 3; in each aligned block of 24 rows (0 to 23, 24 to 47, ...) at most 7 rows name the same one
- col_slot: int32 [768], P(('oi', 'oj')), may hold values from 0 to 23
Outputs:
- new_amplitudes: bfloat16 [768, 128, 128], P(('oi', 'oj'))
- residual: bfloat16 [768, 128, 128], P(('oi', 'oj'))
The draws below stay inside these ranges and needn't reach their ends.
Inputs may be any that keep to these rules, and one draw needn't show every extreme that they name: `row_peer`: among the pairs of one device no index is named by more than 4 pairs, a bound that some block reaches. `col_peer`: among the pairs of one device no index is named by more than 7 pairs, a bound that some block reaches.
All inputs are finite; a program needn't handle non-finite values.
Results may differ from the reference program's by a relative error of at most 0.012.
The reference program's roundings to bfloat16 on the way count: a program that leaves them out, or rounds other values in their place, can miss the bound.
Values may be sent and summed in bfloat16 or wider, within the bound.
A program may use at most 64 MiB of HBM per device.

```python
import math
import jax
import jax.numpy as jnp
import numpy as np
from jax import lax

PNO = 128
NOCC = 20000
P_DEV = 24
ITERS = 3
CAP_ROW = 4
CAP_COL = 7
PAIRS = 768
N_OI = 4
N_OJ = 8


def plant(entries, stream_key, low, high):
    longest = entries.shape.index(max(entries.shape))
    spots = []
    for shift in (0, 1):
        where = [jax.random.randint(jax.random.fold_in(stream_key, axis), (), 0, length) for axis, length in enumerate(entries.shape)]
        where[longest] = (where[longest] + shift) % entries.shape[longest]
        spots.append(tuple(where))
    return entries.at[spots[0]].set(low).at[spots[1]].set(high)


def block_scale(own_key, shape, split, low, high):
    def one(axis_at, parts):
        heights = jax.random.uniform(jax.random.fold_in(jax.random.fold_in(own_key, 6), axis_at), (parts,), jnp.float32, low / len(split), high / len(split))
        return jnp.repeat(jnp.exp(heights), shape[axis_at] // parts).reshape((-1,) + (1,) * (len(shape) - axis_at - 1))

    gain = one(*split[0])
    for cut in split[1:]:
        gain = gain * one(*cut)
    return gain


def assign_block(own_key, own, number, rows, count, top, limit, slope):
    order = jax.random.permutation(own_key, count)
    heavy_load, usual = portions_of(count, rows * top, limit, slope, True), portions_of(count, rows * top, limit, slope, False)
    places = jnp.arange(count)

    def named(sizes, offset_by):
        used = int((sizes > 0).sum())
        fixed = max(1, used // 4)
        passed = fixed + (places - fixed + offset_by * (used - fixed)) % max(1, count - fixed)
        return jnp.zeros((count,), jnp.int32).at[order[jnp.where(places < fixed, places, passed)]].set(jnp.asarray(sizes, jnp.int32))

    sizes = jnp.where(number % 4 == 0, named(heavy_load, number // 4), named(usual, number - number // 4 - 1))
    mixed = jax.random.permutation(jax.random.fold_in(own, 3), count)
    giver, sink = mixed[0:count // 2 * 2:2], mixed[1:count // 2 * 2:2]
    room = jnp.minimum(sizes[giver] - 1, limit - sizes[sink]) // 2
    room = jnp.where((giver == order[0]) | (sink == order[0]) | (sizes[sink] == 0), 0, jnp.maximum(room, 0))
    passed = jax.random.randint(jax.random.fold_in(own, 4), (count // 2,), 0, 1 << 20) % (room + 1)
    sizes = sizes.at[giver].add(-passed).at[sink].add(passed)
    labels = jnp.searchsorted(jnp.cumsum(sizes), jnp.arange(rows * top), side="right").astype(jnp.int32)
    grid = labels.reshape(top, rows).T
    grid = grid[jax.random.permutation(jax.random.fold_in(own, 1), rows)]
    offset_by = jax.random.randint(jax.random.fold_in(own, 2), (rows, 1), 0, top)
    return jnp.take_along_axis(grid, (jnp.arange(top)[None, :] + offset_by) % top, axis=1)


def portions_of(count, total, reach, slope, full):
    portions = [(1 << 20) // math.isqrt(grade ** slope) + 1 for grade in range(1, count + 1)]
    largest = reach if full else min(reach, max(-(-total // count), total * portions[0] // sum(portions)))
    least = 1 if total - largest >= count - 1 else 0
    holding, rest = [largest] + [least] * (count - 1), total - largest - least * (count - 1)
    while rest > 0:
        free = [i for i in range(1, count) if holding[i] < largest] or [i for i in range(1, count) if holding[i] < reach]
        pool, left = sum([portions[i] for i in free]), rest
        for i in free:
            more = min(reach - holding[i], max(1, left * portions[i] // pool), rest)
            holding[i] = holding[i] + more
            rest = rest - more
    return np.array(holding)


def normal_values(own_key, dims, scale, bound, split=(), held_as=jnp.bfloat16):
    gain = block_scale(own_key, dims, split, -0.22, 0.18) if split else 1.0
    values = jax.random.normal(own_key, dims, jnp.float32) * scale * gain
    return jnp.minimum(jnp.maximum(values, -bound), bound).astype(held_as)


def setup_inputs(seed: int = 0) -> dict:
    key_of = jax.random.split(jax.random.key(seed), 14)
    amplitudes = normal_values(key_of[0], (PAIRS, PNO, PNO), 1.0, 6.0, ((0, 32),))
    exchange_ints = normal_values(key_of[1], (PAIRS, PNO, PNO), 1.0, 6.0, ((0, 32),))
    row_intersection = normal_values(key_of[2], (PAIRS, PNO, PNO), PNO ** -0.5, 0.5, ((0, 32),))
    col_intersection = normal_values(key_of[3], (PAIRS, PNO, PNO), PNO ** -0.5, 0.5, ((0, 32),))
    pno_energy = jnp.clip(jnp.exp(math.log(1.0) - 1.609438 * jax.random.uniform(key_of[4], (PAIRS, PNO), jnp.float32) ** block_scale(key_of[4], (PAIRS, PNO), ((0, 32),), -0.2, 0.2)), 0.2, 1.0)
    row_fock = jnp.clip(jax.random.uniform(key_of[5], (PAIRS,), jnp.float32, -1.0, 1.0) * block_scale(key_of[5], (PAIRS,), ((0, 32),), -0.4, 0.0), -1.0, 1.0)
    col_fock = jnp.clip(jax.random.uniform(key_of[6], (PAIRS,), jnp.float32, -1.0, 1.0) * block_scale(key_of[6], (PAIRS,), ((0, 32),), -0.4, 0.0), -1.0, 1.0)
    pair_occ = plant(jax.random.randint(key_of[7], (PAIRS, 2), 0, NOCC), jax.random.fold_in(key_of[7], 1), 0, NOCC - 1).astype(jnp.int32)
    fock_occ = jnp.clip(jax.random.uniform(key_of[8], (NOCC,), jnp.float32, -0.6, -0.2), -0.6, -0.2)
    row_peer_keys = jax.random.split(jax.random.fold_in(key_of[9], 1), PAIRS // P_DEV)
    row_peer_turns = jax.random.permutation(jax.random.fold_in(key_of[9], 3), PAIRS // P_DEV)
    row_peer = jax.vmap(lambda own, number: assign_block(jax.random.fold_in(key_of[9], 2), own, number, P_DEV, N_OJ, 1, CAP_ROW, 2))(row_peer_keys, row_peer_turns).reshape((PAIRS, 1))
    row_slot = plant(jax.random.randint(key_of[10], (PAIRS,), 0, P_DEV), jax.random.fold_in(key_of[10], 1), 0, P_DEV - 1).astype(jnp.int32)
    col_peer_keys = jax.random.split(jax.random.fold_in(key_of[11], 1), PAIRS // P_DEV)
    col_peer_turns = jax.random.permutation(jax.random.fold_in(key_of[11], 3), PAIRS // P_DEV)
    col_peer = jax.vmap(lambda own, number: assign_block(jax.random.fold_in(key_of[11], 2), own, number, P_DEV, N_OI, 1, CAP_COL, 2))(col_peer_keys, col_peer_turns).reshape((PAIRS, 1))
    col_slot = plant(jax.random.randint(key_of[12], (PAIRS,), 0, P_DEV), jax.random.fold_in(key_of[12], 1), 0, P_DEV - 1).astype(jnp.int32)
    return {"amplitudes": amplitudes, "exchange_ints": exchange_ints, "row_intersection": row_intersection, "col_intersection": col_intersection, "pno_energy": pno_energy, "row_fock": row_fock, "col_fock": col_fock, "pair_occ": pair_occ, "fock_occ": fock_occ, "row_peer": row_peer, "row_slot": row_slot, "col_peer": col_peer, "col_slot": col_slot}


def couple(blocks, intersection):
    first = jnp.einsum('pab,pbc->pac', intersection.astype(jnp.float32), blocks.astype(jnp.float32)).astype(jnp.bfloat16)
    return jnp.einsum('pac,pdc->pad', first.astype(jnp.float32), intersection.astype(jnp.float32))


def reference(amplitudes, exchange_ints, row_intersection, col_intersection, pno_energy, row_fock, col_fock, pair_occ, fock_occ, row_peer, row_slot, col_peer, col_slot):
    pair_ids = jnp.arange(PAIRS, dtype=jnp.int32)
    device = pair_ids // P_DEV
    row_source = (((device // N_OJ) * N_OJ + row_peer[:, 0]) * P_DEV + row_slot).astype(jnp.int32)
    col_source = ((col_peer[:, 0] * N_OJ + device % N_OJ) * P_DEV + col_slot).astype(jnp.int32)
    occupied = fock_occ[pair_occ[:, 0]] + fock_occ[pair_occ[:, 1]]

    def shaped(array):
        return array.reshape((N_OI * N_OJ, P_DEV) + array.shape[1:])

    stacked = tuple(shaped(array) for array in (exchange_ints, row_intersection, col_intersection, pno_energy, occupied, row_fock, col_fock, row_source, col_source))
    residual = jnp.zeros((PAIRS, PNO, PNO), jnp.bfloat16)
    for sweep in range(ITERS):
        current = amplitudes

        def one_device(item):
            ints, row_over, col_over, energy, occ_sum, row_coef, col_coef, row_from, col_from, own = item
            denominator = energy[:, :, None] + energy[:, None, :] - occ_sum[:, None, None]
            row_term = couple(current[row_from], row_over)
            col_term = couple(current[col_from], col_over)
            sweep_residual = ints.astype(jnp.float32) + denominator * own.astype(jnp.float32) - row_coef[:, None, None] * row_term - col_coef[:, None, None] * col_term
            updated = (own.astype(jnp.float32) - sweep_residual / denominator).astype(jnp.bfloat16)
            return updated, sweep_residual.astype(jnp.bfloat16)

        updated, rounded = lax.map(one_device, stacked + (shaped(amplitudes),))
        amplitudes = updated.reshape(PAIRS, PNO, PNO)
        residual = rounded.reshape(PAIRS, PNO, PNO)
    return amplitudes, residual
```

```python
import functools
import jax
import jax.numpy as jnp
from jax import lax
from jax.experimental import pallas as pl
from jax.experimental.pallas import tpu as pltpu
from jax.sharding import PartitionSpec as P

ITERS = 3
LANES = 128
PERM, PLACE, ROW_FROM = 0, 1, 2


def flip(me, step):
    out = me
    bit = 1
    while bit <= step:
        if step & bit:
            out = out + bit * (1 - 2 * ((me // bit) % 2))
        bit *= 2
    return out


def plan_kernel(
    rows, cols, row_cap, col_cap, row_peer, row_slot, col_peer, col_slot, table, meta, count
):
    pairs = row_peer.shape[0]
    row_me, col_me = lax.axis_index("oj"), lax.axis_index("oi")
    for g in range(rows + cols):
        count[g] = 0
        for t in range(row_cap if g < rows else col_cap):
            table[g, 0, t] = 0
    for k in range(cols * col_cap):
        meta[PERM, k] = 0
        meta[ROW_FROM, k] = 0

    @pl.loop(0, pairs)
    def _(p):
        g = row_peer[p] ^ row_me
        t = count[g]
        count[g] = t + 1
        table[g, 0, t] = row_slot[p]
        h = col_peer[p] ^ col_me
        u = count[rows + h]
        count[rows + h] = u + 1
        table[rows + h, 0, u] = col_slot[p]
        place = h * col_cap + u
        meta[PERM, place] = p
        meta[PLACE, p] = place
        meta[ROW_FROM, place] = g * row_cap + t


def sweep_kernel(
    rows,
    cols,
    row_cap,
    col_cap,
    table,
    amps,
    meta,
    row_fock,
    col_fock,
    pair_occ,
    fock_hbm,
    ints_hbm,
    row_over_hbm,
    col_over_hbm,
    energy,
    new_out,
    res_out,
    fock,
    ints,
    row_over,
    col_over,
    want_in,
    want,
    denom,
    inverse,
    partial,
    current,
    res_sorted,
    row_got_0,
    row_got_1,
    row_got_2,
    col_got,
    row_send,
    col_send,
    local_sem,
    table_send_sem,
    table_recv_sem,
    send_sem,
    recv_sem,
):
    row_got = (row_got_0, row_got_1, row_got_2)
    places = cols * col_cap
    pairs = amps.shape[0]
    width = amps.shape[1]
    row_me, col_me = lax.axis_index("oj"), lax.axis_index("oi")
    groups = [g for g in range(rows + cols) if g not in (0, rows)]

    def peer(g):
        if g < rows:
            return {"oj": flip(row_me, g)}
        return {"oi": flip(col_me, g - rows)}

    loads = [
        pltpu.make_async_copy(source, target, local_sem.at[i])
        for i, (source, target) in enumerate(
            [
                (ints_hbm, ints),
                (row_over_hbm, row_over),
                (col_over_hbm, col_over),
                (fock_hbm, fock),
            ]
        )
    ]
    barrier = pltpu.get_barrier_semaphore()
    for g in groups:
        pl.semaphore_signal(
            barrier, inc=1, device_id=peer(g), device_id_type=pl.DeviceIdType.MESH
        )
    for load in loads:
        load.start()
    want_in[0] = table[0]
    want_in[rows] = table[rows]
    pl.semaphore_wait(barrier, len(groups))
    asks = []
    for g in groups:
        ask = pltpu.make_async_remote_copy(
            src_ref=table.at[g],
            dst_ref=want_in.at[g],
            send_sem=table_send_sem.at[g],
            recv_sem=table_recv_sem.at[g],
            device_id=peer(g),
            device_id_type=pl.DeviceIdType.MESH,
        )
        ask.start()
        asks.append(ask)
    for ask in asks:
        ask.wait()
    move = pltpu.make_async_copy(want_in, want, local_sem.at[4])
    move.start()
    move.wait()

    def block_copy(sweep, g):
        if g < rows:
            here = pl.ds(g * row_cap, row_cap)
            source, target = row_send.at[sweep, here], row_got[sweep].at[here]
        else:
            here = pl.ds((g - rows) * col_cap, col_cap)
            source, target = col_send.at[sweep, here], col_got.at[sweep, here]
        return pltpu.make_async_remote_copy(
            src_ref=source,
            dst_ref=target,
            send_sem=send_sem.at[sweep, g],
            recv_sem=recv_sem.at[sweep, g],
            device_id=peer(g),
            device_id_type=pl.DeviceIdType.MESH,
        )

    def dot(a, b, contract):
        return lax.dot_general(
            a, b, (((1,), (contract,)), ((), ())), preferred_element_type=jnp.float32
        )

    def couple(blocks, overs):
        firsts = [dot(o, b, 0).astype(jnp.bfloat16) for o, b in zip(overs, blocks)]
        return [dot(f, o, 1) for f, o in zip(firsts, overs)]

    order = list(range(rows + cols - 1, rows, -1)) + list(range(rows - 1, 0, -1)) + [rows, 0]
    for sweep in range(ITERS):
        held = (sweep + 1) % 2

        def taken(slot):
            if sweep == 0:
                return amps[slot]
            return current[held, meta[PLACE, slot]]

        for g in order:
            if g < rows:
                first, cap, out, got = g * row_cap, row_cap, row_send, row_got[sweep]
            else:
                first, cap, out, got = (g - rows) * col_cap, col_cap, col_send, col_got.at[sweep]
            out = got if g in (0, rows) else out.at[sweep]
            for t in range(cap):
                out[first + t] = taken(want[g, 0, t])
            if g not in (0, rows):
                block_copy(sweep, g).start()

        if sweep == 0:
            for load in loads:
                load.wait()

            @pl.loop(0, places)
            def _(k):
                p = meta[PERM, k]
                occupied = fock[pair_occ[2 * p]] + fock[pair_occ[2 * p + 1]]
                across = jnp.broadcast_to(energy[p], (width, width))
                value = across + across.T - occupied
                denom[k] = value
                inverse[k] = 1.0 / value

        for g in range(1, rows):
            block_copy(sweep, g).wait_recv()

        @pl.loop(0, cols)
        def _(h):
            at = [h * col_cap + t for t in range(col_cap)]
            who = [meta[PERM, k] for k in at]
            overs = [row_over[p] for p in who]
            blocks = [row_got[sweep][meta[ROW_FROM, k]] for k in at]
            for k, p, term in zip(at, who, couple(blocks, overs)):
                partial[k] = row_fock[p] * term - ints[p].astype(jnp.float32)

        def col_group(h):
            at = [h * col_cap + t for t in range(col_cap)]
            who = [meta[PERM, k] for k in at]
            overs = [col_over[p] for p in who]
            blocks = [col_got[sweep, k] for k in at]
            for k, p, term in zip(at, who, couple(blocks, overs)):
                total = partial[k] + col_fock[p] * term
                if sweep == ITERS - 1:
                    own = current[held, k].astype(jnp.float32)
                    res_sorted[k] = (denom[k] * own - total).astype(jnp.bfloat16)
                current[sweep % 2, k] = (total * inverse[k]).astype(jnp.bfloat16)

        col_group(0)

        @pl.loop(1, cols)
        def _(h):
            here = pl.ds(h * col_cap, col_cap)
            pltpu.make_async_remote_copy(
                src_ref=col_send.at[sweep, here],
                dst_ref=col_got.at[sweep, here],
                send_sem=send_sem.at[sweep, rows + h],
                recv_sem=recv_sem.at[sweep, rows + h],
                device_id={"oi": flip(col_me, 1)},
                device_id_type=pl.DeviceIdType.MESH,
            ).wait_recv()
            col_group(h)

    for p in range(pairs):
        place = meta[PLACE, p]
        new_out[p] = current[(ITERS - 1) % 2, place]
        res_out[p] = res_sorted[place]
    for sweep in range(ITERS):
        for g in groups:
            block_copy(sweep, g).wait_send()


def body(
    amplitudes,
    exchange_ints,
    row_intersection,
    col_intersection,
    pno_energy,
    row_fock,
    col_fock,
    pair_occ,
    fock_occ,
    row_peer,
    row_slot,
    col_peer,
    col_slot,
):
    pairs, width, _ = amplitudes.shape
    rows, cols = lax.axis_size("oj"), lax.axis_size("oi")
    row_cap = max(2, (pairs + rows - 1) // rows + 1)
    col_cap = max(2, (pairs + cols - 1) // cols + 1)
    places = cols * col_cap
    smem = pl.BlockSpec(memory_space=pltpu.SMEM)
    vmem = pl.BlockSpec(memory_space=pltpu.VMEM)
    anywhere = pl.BlockSpec(memory_space=pl.ANY)
    table, meta = pl.pallas_call(
        functools.partial(plan_kernel, rows, cols, row_cap, col_cap),
        out_shape=(
            jax.ShapeDtypeStruct((rows + cols, 1, LANES), jnp.int32),
            jax.ShapeDtypeStruct((3, LANES), jnp.int32),
        ),
        in_specs=[smem] * 4,
        out_specs=(smem, smem),
        scratch_shapes=[pltpu.SMEM((rows + cols,), jnp.int32)],
        name="plan",
    )(row_peer.reshape(-1), row_slot, col_peer.reshape(-1), col_slot)
    wide = jax.ShapeDtypeStruct(amplitudes.shape, jnp.bfloat16)
    block = (width, width)
    half, full = jnp.bfloat16, jnp.float32
    return pl.pallas_call(
        functools.partial(sweep_kernel, rows, cols, row_cap, col_cap),
        out_shape=(wide, wide),
        in_specs=[vmem, vmem, smem, smem, smem, smem, anywhere, anywhere, anywhere, anywhere, vmem],
        out_specs=(vmem, vmem),
        scratch_shapes=[
            pltpu.SMEM(fock_occ.shape, full),
            pltpu.VMEM(amplitudes.shape, half),
            pltpu.VMEM(amplitudes.shape, half),
            pltpu.VMEM(amplitudes.shape, half),
            pltpu.VMEM((rows + cols, 1, LANES), jnp.int32),
            pltpu.SMEM((rows + cols, 1, LANES), jnp.int32),
            pltpu.VMEM((places,) + block, full),
            pltpu.VMEM((places,) + block, full),
            pltpu.VMEM((places,) + block, full),
            pltpu.VMEM((2, places) + block, half),
            pltpu.VMEM((places,) + block, half),
            pltpu.VMEM((rows * row_cap,) + block, half),
            pltpu.VMEM((rows * row_cap,) + block, half),
            pltpu.VMEM((rows * row_cap,) + block, half),
            pltpu.VMEM((ITERS, places) + block, half),
            pltpu.VMEM((ITERS, rows * row_cap) + block, half),
            pltpu.VMEM((ITERS, places) + block, half),
            pltpu.SemaphoreType.DMA((5,)),
            pltpu.SemaphoreType.DMA((rows + cols,)),
            pltpu.SemaphoreType.DMA((rows + cols,)),
            pltpu.SemaphoreType.DMA((ITERS, rows + cols)),
            pltpu.SemaphoreType.DMA((ITERS, rows + cols)),
        ],
        compiler_params=pltpu.CompilerParams(
            collective_id=0, has_side_effects=True, vmem_limit_bytes=52 * 1024 * 1024
        ),
        name="sweeps",
    )(
        table,
        amplitudes,
        meta,
        row_fock,
        col_fock,
        pair_occ.reshape(-1),
        fock_occ,
        exchange_ints,
        row_intersection,
        col_intersection,
        pno_energy.reshape(pairs, 1, width),
    )


def solution(mesh):
    return jax.shard_map(
        body,
        mesh=mesh,
        in_specs=(
            P(("oi", "oj"), None, None),
            P(("oi", "oj"), None, None),
            P(("oi", "oj"), None, None),
            P(("oi", "oj"), None, None),
            P(("oi", "oj"), None),
            P(("oi", "oj")),
            P(("oi", "oj")),
            P(("oi", "oj"), None),
            P(),
            P(("oi", "oj"), None),
            P(("oi", "oj")),
            P(("oi", "oj"), None),
            P(("oi", "oj")),
        ),
        out_specs=(P(("oi", "oj"), None, None), P(("oi", "oj"), None, None)),
        check_vma=False,
    )
```

```python
import functools
import jax
import jax.numpy as jnp
from jax import lax
from jax.experimental import pallas as pl
from jax.experimental.pallas import tpu as pltpu
from jax.sharding import PartitionSpec as P

ITERS = 3
LANES = 128


def flip(me, step):
    out = me
    bit = 1
    while bit <= step:
        if step & bit:
            out = out + bit * (1 - 2 * ((me // bit) % 2))
        bit *= 2
    return out


def grouped(peer, me):
    group = (peer ^ me).astype(jnp.float32)
    along = jnp.broadcast_to(group, (LANES, LANES))
    earlier = lax.broadcasted_iota(jnp.int32, (LANES, LANES), 0) < lax.broadcasted_iota(
        jnp.int32, (LANES, LANES), 1
    )
    same = jnp.where((along.T == along) & earlier, 1.0, 0.0)
    return group, jnp.sum(same, axis=0, keepdims=True)


def bounded(values, count):
    return jnp.minimum(jnp.maximum(values.astype(jnp.int32), 0), count - 1)


def listed(group, before, values, count, cap, pairs):
    tall = -(-count // 8) * 8
    which = lax.broadcasted_iota(jnp.int32, (tall, LANES), 0).astype(jnp.float32)
    lane = lax.broadcasted_iota(jnp.int32, (tall, LANES), 1)
    mine = group == which
    out = jnp.zeros((tall, LANES), jnp.float32)
    for t in range(cap):
        one = jnp.sum(jnp.where(mine & (before == t), values, 0.0), axis=1, keepdims=True)
        out = jnp.where(lane == t, one, out)
    return bounded(out, pairs)


def sweep_kernel(
    rows,
    cols,
    row_cap,
    col_cap,
    row_peer_hbm,
    row_slot_hbm,
    col_peer_hbm,
    col_slot_hbm,
    amps_hbm,
    row_fock_hbm,
    col_fock_hbm,
    pair_occ_hbm,
    fock_hbm,
    ints_hbm,
    row_over_hbm,
    col_over_hbm,
    energy_hbm,
    new_out,
    res_out,
    short,
    long,
    table,
    places_in,
    meta,
    row_fock,
    col_fock,
    pair_occ,
    fock,
    amps,
    ints,
    row_over,
    col_over,
    energy,
    want_in,
    want,
    denom,
    inverse,
    partial,
    current,
    res_sorted,
    row_got_0,
    row_got_1,
    row_got_2,
    col_got,
    row_send,
    col_send,
    local_sem,
    table_send_sem,
    table_recv_sem,
    row_send_sem,
    row_recv_sem,
    col_send_sem,
    col_recv_sem,
):
    row_got = (row_got_0, row_got_1, row_got_2)
    places = cols * col_cap
    pairs = amps.shape[0]
    width = amps.shape[1]
    row_me, col_me = lax.axis_index("oj"), lax.axis_index("oi")
    groups = [g for g in range(rows + cols) if g not in (0, rows)]
    place_at, from_at = cols, cols + 1

    def peer(g):
        if g < rows:
            return {"oj": flip(row_me, g)}
        return {"oi": flip(col_me, g - rows)}

    def local(source, target, i):
        return pltpu.make_async_copy(source, target, local_sem.at[i])

    small = [
        local(source, short.at[i], i)
        for i, source in enumerate((row_peer_hbm, row_slot_hbm, col_peer_hbm, col_slot_hbm))
    ]
    first_load = local(amps_hbm, amps, 4)
    loads = [
        local(source, target, 5 + i)
        for i, (source, target) in enumerate(
            (
                (energy_hbm, energy),
                (row_fock_hbm, row_fock),
                (col_fock_hbm, col_fock),
                (pair_occ_hbm, pair_occ),
                (fock_hbm, fock),
                (row_over_hbm, row_over),
                (col_over_hbm, col_over),
                (ints_hbm, ints),
            )
        )
    ]
    for load in small:
        load.start()
    barrier = pltpu.get_barrier_semaphore()
    for g in groups:
        pl.semaphore_signal(
            barrier, inc=1, device_id=peer(g), device_id_type=pl.DeviceIdType.MESH
        )
    first_load.start()
    for load in loads:
        load.start()
    long[...] = jnp.full(long.shape, 1 << 20, jnp.int32)
    for load in small:
        load.wait()
    for i in range(4):
        long[i, :, 0:pairs] = short[i]
    row_group, row_before = grouped(long[0], row_me)
    col_group_of, col_before = grouped(long[2], col_me)
    row_asked = listed(row_group, row_before, long[1].astype(jnp.float32), rows, row_cap, pairs)
    col_asked = listed(col_group_of, col_before, long[3].astype(jnp.float32), cols, col_cap, pairs)
    for g in range(rows):
        table[g] = row_asked[g : g + 1]
    for g in range(cols):
        table[rows + g] = col_asked[g : g + 1]
    pl.semaphore_wait(barrier, len(groups))
    asks = []
    for g in groups:
        ask = pltpu.make_async_remote_copy(
            src_ref=table.at[g],
            dst_ref=want_in.at[g],
            send_sem=table_send_sem.at[g],
            recv_sem=table_recv_sem.at[g],
            device_id=peer(g),
            device_id_type=pl.DeviceIdType.MESH,
        )
        ask.start()
        asks.append(ask)
    want_in[0] = table[0]
    want_in[rows] = table[rows]
    pair_ids = lax.broadcasted_iota(jnp.int32, (1, LANES), 1).astype(jnp.float32)
    order = listed(col_group_of, col_before, pair_ids, cols, col_cap, pairs)
    for h in range(cols):
        places_in[h] = order[h : h + 1]
    places_in[place_at] = bounded(col_group_of * col_cap + col_before, places)
    places_in[from_at] = bounded(row_group * row_cap + row_before, rows * row_cap)
    move_places = local(places_in, meta, 13)
    move_places.start()
    move_places.wait()
    first_load.wait()
    for ask in asks:
        ask.wait()
    move = local(want_in, want, 14)
    move.start()
    move.wait()

    def row_copy(sweep, g):
        here = pl.ds(g * row_cap, row_cap)
        return pltpu.make_async_remote_copy(
            src_ref=row_send.at[sweep, here],
            dst_ref=row_got[sweep].at[here],
            send_sem=row_send_sem.at[sweep, g],
            recv_sem=row_recv_sem.at[sweep, g],
            device_id=peer(g),
            device_id_type=pl.DeviceIdType.MESH,
        )

    def col_copy(sweep, h, t):
        here = pl.ds(h * col_cap + t, 1)
        return pltpu.make_async_remote_copy(
            src_ref=col_send.at[sweep, here],
            dst_ref=col_got.at[sweep, here],
            send_sem=col_send_sem.at[sweep, h * col_cap + t],
            recv_sem=col_recv_sem.at[sweep, h * col_cap + t],
            device_id=peer(rows + h),
            device_id_type=pl.DeviceIdType.MESH,
        )

    def wait_sent(sweep):
        for g in range(1, rows):
            row_copy(sweep, g).wait_send()
        for h in range(1, cols):
            for t in range(col_cap):
                col_copy(sweep, h, t).wait_send()

    def dot(a, b, contract):
        return lax.dot_general(
            a, b, (((1,), (contract,)), ((), ())), preferred_element_type=jnp.float32
        )

    def couple(blocks, overs):
        firsts = [dot(o, b, 0).astype(jnp.bfloat16) for o, b in zip(overs, blocks)]
        return [dot(f, o, 1) for f, o in zip(firsts, overs)]

    for sweep in range(ITERS):
        held = (sweep + 1) % 2

        def taken(slot):
            if sweep == 0:
                return amps[slot]
            return current[held, meta[place_at, 0, slot]]

        def send_rows(g):
            for t in range(row_cap):
                row_send[sweep, g * row_cap + t] = taken(want[g, 0, t])
            row_copy(sweep, g).start()

        row_next = 1
        for t in range(col_cap):
            for h in range(cols - 1, 0, -1):
                col_send[sweep, h * col_cap + t] = taken(want[rows + h, 0, t])
                col_copy(sweep, h, t).start()
            row_end = 1 + (rows - 1) * (t + 1) // col_cap
            for g in range(row_next, row_end):
                send_rows(g)
            row_next = row_end
        for t in range(col_cap):
            col_got[sweep, t] = taken(want[rows, 0, t])
        for t in range(row_cap):
            row_got[sweep][t] = taken(want[0, 0, t])

        if sweep == 0:
            for load in loads:
                load.wait()

            @pl.loop(0, cols)
            def _(h):
                for t in range(col_cap):
                    p = meta[h, 0, t]
                    occupied = fock[pair_occ[0, p]] + fock[pair_occ[1, p]]
                    across = jnp.broadcast_to(energy[p], (width, width))
                    value = across + across.T - occupied
                    denom[h * col_cap + t] = value
                    inverse[h * col_cap + t] = 1.0 / value
        else:
            wait_sent(sweep - 1)

        for g in range(1, rows):
            row_copy(sweep, g).wait_recv()

        @pl.loop(0, cols)
        def _(h):
            who = [meta[h, 0, t] for t in range(col_cap)]
            overs = [row_over[p] for p in who]
            blocks = [row_got[sweep][meta[from_at, 0, p]] for p in who]
            for t, (p, term) in enumerate(zip(who, couple(blocks, overs))):
                partial[h * col_cap + t] = row_fock[p] * term - ints[p].astype(jnp.float32)

        def col_part(at):
            who = [meta[h, 0, t] for h, t in at]
            overs = [col_over[p] for p in who]
            keys = [h * col_cap + t for h, t in at]
            blocks = [col_got[sweep, k] for k in keys]
            for k, p, term in zip(keys, who, couple(blocks, overs)):
                total = partial[k] + col_fock[p] * term
                if sweep == ITERS - 1:
                    own = current[held, k].astype(jnp.float32)
                    res_sorted[k] = (denom[k] * own - total).astype(jnp.bfloat16)
                current[sweep % 2, k] = (total * inverse[k]).astype(jnp.bfloat16)

        near = min(2, cols)
        for h in range(near):
            if h:
                for t in range(col_cap):
                    col_copy(sweep, h, t).wait_recv()
            col_part([(h, t) for t in range(col_cap)])
        for t in range(col_cap):
            for h in range(near, cols):
                col_copy(sweep, h, t).wait_recv()
            col_part([(h, t) for h in range(near, cols)])

    for p in range(pairs):
        place = meta[place_at, 0, p]
        new_out[p] = current[(ITERS - 1) % 2, place]
        res_out[p] = res_sorted[place]
    wait_sent(ITERS - 1)


def body(
    amplitudes,
    exchange_ints,
    row_intersection,
    col_intersection,
    pno_energy,
    row_fock,
    col_fock,
    pair_occ,
    fock_occ,
    row_peer,
    row_slot,
    col_peer,
    col_slot,
):
    pairs, width, _ = amplitudes.shape
    rows, cols = lax.axis_size("oj"), lax.axis_size("oi")
    row_cap = max(2, (pairs + rows - 1) // rows + 1)
    col_cap = max(2, (pairs + cols - 1) // cols + 1)
    places = cols * col_cap
    wide = jax.ShapeDtypeStruct(amplitudes.shape, jnp.bfloat16)
    block = (width, width)
    half, full, whole = jnp.bfloat16, jnp.float32, jnp.int32
    vmem, smem = pltpu.VMEM, pltpu.SMEM
    return pl.pallas_call(
        functools.partial(sweep_kernel, rows, cols, row_cap, col_cap),
        out_shape=(wide, wide),
        in_specs=[pl.BlockSpec(memory_space=pltpu.HBM)] * 13,
        out_specs=(pl.BlockSpec(memory_space=vmem),) * 2,
        scratch_shapes=[
            vmem((4, 1, pairs), whole),
            vmem((4, 1, LANES), whole),
            vmem((rows + cols, 1, LANES), whole),
            vmem((cols + 2, 1, LANES), whole),
            smem((cols + 2, 1, LANES), whole),
            smem((pairs,), full),
            smem((pairs,), full),
            smem((2, pairs), whole),
            smem(fock_occ.shape, full),
            vmem(amplitudes.shape, half),
            vmem(amplitudes.shape, half),
            vmem(amplitudes.shape, half),
            vmem(amplitudes.shape, half),
            vmem((pairs, 1, width), full),
            vmem((rows + cols, 1, LANES), whole),
            smem((rows + cols, 1, LANES), whole),
            vmem((places,) + block, full),
            vmem((places,) + block, full),
            vmem((places,) + block, full),
            vmem((2, places) + block, half),
            vmem((places,) + block, half),
            vmem((rows * row_cap,) + block, half),
            vmem((rows * row_cap,) + block, half),
            vmem((rows * row_cap,) + block, half),
            vmem((ITERS, places) + block, half),
            vmem((ITERS, rows * row_cap) + block, half),
            vmem((ITERS, places) + block, half),
            pltpu.SemaphoreType.DMA((15,)),
            pltpu.SemaphoreType.DMA((rows + cols,)),
            pltpu.SemaphoreType.DMA((rows + cols,)),
            pltpu.SemaphoreType.DMA((ITERS, rows)),
            pltpu.SemaphoreType.DMA((ITERS, rows)),
            pltpu.SemaphoreType.DMA((ITERS, places)),
            pltpu.SemaphoreType.DMA((ITERS, places)),
        ],
        compiler_params=pltpu.CompilerParams(
            collective_id=0, has_side_effects=True, vmem_limit_bytes=60 * 1024 * 1024
        ),
        name="sweeps",
    )(
        row_peer.reshape(1, pairs),
        row_slot.reshape(1, pairs),
        col_peer.reshape(1, pairs),
        col_slot.reshape(1, pairs),
        amplitudes,
        row_fock,
        col_fock,
        pair_occ.T,
        fock_occ,
        exchange_ints,
        row_intersection,
        col_intersection,
        pno_energy.reshape(pairs, 1, width),
    )


def solution(mesh):
    return jax.shard_map(
        body,
        mesh=mesh,
        in_specs=(
            P(("oi", "oj"), None, None),
            P(("oi", "oj"), None, None),
            P(("oi", "oj"), None, None),
            P(("oi", "oj"), None, None),
            P(("oi", "oj"), None),
            P(("oi", "oj")),
            P(("oi", "oj")),
            P(("oi", "oj"), None),
            P(),
            P(("oi", "oj"), None),
            P(("oi", "oj")),
            P(("oi", "oj"), None),
            P(("oi", "oj")),
        ),
        out_specs=(P(("oi", "oj"), None, None), P(("oi", "oj"), None, None)),
        check_vma=False,
    )
```

```python
import functools
import jax
import jax.numpy as jnp
from jax import lax
from jax.experimental import pallas as pl
from jax.experimental.pallas import tpu as pltpu
from jax.sharding import PartitionSpec as P

ITERS = 3
LANES = 128


def flip(me, step):
    out = me
    bit = 1
    while bit <= step:
        if step & bit:
            out = out + bit * (1 - 2 * ((me // bit) % 2))
        bit *= 2
    return out


def grouped(peer, me):
    group = (peer ^ me).astype(jnp.float32)
    along = jnp.broadcast_to(group, (LANES, LANES))
    earlier = lax.broadcasted_iota(jnp.int32, (LANES, LANES), 0) < lax.broadcasted_iota(
        jnp.int32, (LANES, LANES), 1
    )
    same = jnp.where((along.T == along) & earlier, 1.0, 0.0)
    return group, jnp.sum(same, axis=0, keepdims=True)


def bounded(values, count):
    return jnp.minimum(jnp.maximum(values.astype(jnp.int32), 0), count - 1)


def listed(group, before, values, count, cap, pairs):
    tall = -(-count // 8) * 8
    which = lax.broadcasted_iota(jnp.int32, (tall, LANES), 0).astype(jnp.float32)
    lane = lax.broadcasted_iota(jnp.int32, (tall, LANES), 1)
    mine = group == which
    out = jnp.zeros((tall, LANES), jnp.float32)
    for t in range(cap):
        one = jnp.sum(jnp.where(mine & (before == t), values, 0.0), axis=1, keepdims=True)
        out = jnp.where(lane == t, one, out)
    return bounded(out, pairs)


def sweep_kernel(
    rows,
    cols,
    row_cap,
    col_cap,
    row_peer_hbm,
    row_slot_hbm,
    col_peer_hbm,
    col_slot_hbm,
    amps_hbm,
    row_fock_hbm,
    col_fock_hbm,
    pair_occ_hbm,
    fock_hbm,
    ints_hbm,
    row_over_hbm,
    col_over_hbm,
    energy_hbm,
    new_out,
    res_out,
    short,
    long,
    table,
    places_in,
    meta,
    row_fock,
    col_fock,
    pair_occ,
    fock,
    amps,
    ints,
    row_over,
    col_over,
    energy,
    want_in,
    want,
    denom,
    inverse,
    partial,
    current,
    res_sorted,
    row_got_0,
    row_got_1,
    row_got_2,
    col_got,
    row_send,
    col_send,
    local_sem,
    table_send_sem,
    table_recv_sem,
    row_send_sem,
    row_recv_sem,
    col_send_sem,
    col_recv_sem,
):
    row_got = (row_got_0, row_got_1, row_got_2)
    places = cols * col_cap
    pairs = amps.shape[0]
    width = amps.shape[1]
    row_me, col_me = lax.axis_index("oj"), lax.axis_index("oi")
    groups = [g for g in range(rows + cols) if g not in (0, rows)]
    place_at, from_at = cols, cols + 1

    def peer(g):
        if g < rows:
            return {"oj": flip(row_me, g)}
        return {"oi": flip(col_me, g - rows)}

    def local(source, target, i):
        return pltpu.make_async_copy(source, target, local_sem.at[i])

    small = [
        local(source, short.at[i], i)
        for i, source in enumerate((row_peer_hbm, row_slot_hbm, col_peer_hbm, col_slot_hbm))
    ]
    first_load = local(amps_hbm, amps, 4)
    loads = [
        local(source, target, 5 + i)
        for i, (source, target) in enumerate(
            (
                (energy_hbm, energy),
                (row_fock_hbm, row_fock),
                (col_fock_hbm, col_fock),
                (pair_occ_hbm, pair_occ),
                (fock_hbm, fock),
                (row_over_hbm, row_over),
                (col_over_hbm, col_over),
                (ints_hbm, ints),
            )
        )
    ]
    for load in small:
        load.start()
    barrier = pltpu.get_barrier_semaphore()
    for g in groups:
        pl.semaphore_signal(
            barrier, inc=1, device_id=peer(g), device_id_type=pl.DeviceIdType.MESH
        )
    first_load.start()
    for load in loads:
        load.start()
    long[...] = jnp.full(long.shape, 1 << 20, jnp.int32)
    for load in small:
        load.wait()
    for i in range(4):
        long[i, :, 0:pairs] = short[i]
    col_group_of, col_before = grouped(long[2], col_me)
    col_asked = listed(col_group_of, col_before, long[3].astype(jnp.float32), cols, col_cap, pairs)
    for g in range(cols):
        table[rows + g] = col_asked[g : g + 1]

    def ask(g):
        return pltpu.make_async_remote_copy(
            src_ref=table.at[g],
            dst_ref=want_in.at[g],
            send_sem=table_send_sem.at[g],
            recv_sem=table_recv_sem.at[g],
            device_id=peer(g),
            device_id_type=pl.DeviceIdType.MESH,
        )

    pl.semaphore_wait(barrier, len(groups))
    for g in range(rows + 1, rows + cols):
        ask(g).start()
    row_group, row_before = grouped(long[0], row_me)
    row_asked = listed(row_group, row_before, long[1].astype(jnp.float32), rows, row_cap, pairs)
    for g in range(rows):
        table[g] = row_asked[g : g + 1]
    for g in range(1, rows):
        ask(g).start()
    want_in[0] = table[0]
    want_in[rows] = table[rows]
    first_load.wait()

    def take_asked(first, count, i):
        for g in range(first + 1, first + count):
            ask(g).wait()
        here = pl.ds(first, count)
        move = local(want_in.at[here], want.at[here], i)
        move.start()
        return move

    take_asked(rows, cols, 14).wait()

    def place_pairs():
        pair_ids = lax.broadcasted_iota(jnp.int32, (1, LANES), 1).astype(jnp.float32)
        order = listed(col_group_of, col_before, pair_ids, cols, col_cap, pairs)
        for h in range(cols):
            places_in[h] = order[h : h + 1]
        places_in[place_at] = bounded(col_group_of * col_cap + col_before, places)
        places_in[from_at] = bounded(row_group * row_cap + row_before, rows * row_cap)
        move = local(places_in, meta, 13)
        move.start()
        return move

    def row_copy(sweep, g):
        here = pl.ds(g * row_cap, row_cap)
        return pltpu.make_async_remote_copy(
            src_ref=row_send.at[sweep, here],
            dst_ref=row_got[sweep].at[here],
            send_sem=row_send_sem.at[sweep, g],
            recv_sem=row_recv_sem.at[sweep, g],
            device_id=peer(g),
            device_id_type=pl.DeviceIdType.MESH,
        )

    def col_copy(sweep, h, t):
        here = pl.ds(h * col_cap + t, 1)
        return pltpu.make_async_remote_copy(
            src_ref=col_send.at[sweep, here],
            dst_ref=col_got.at[sweep, here],
            send_sem=col_send_sem.at[sweep, h * col_cap + t],
            recv_sem=col_recv_sem.at[sweep, h * col_cap + t],
            device_id=peer(rows + h),
            device_id_type=pl.DeviceIdType.MESH,
        )

    def wait_sent(sweep):
        for g in range(1, rows):
            row_copy(sweep, g).wait_send()
        for h in range(1, cols):
            for t in range(col_cap):
                col_copy(sweep, h, t).wait_send()

    def dot(a, b, contract):
        return lax.dot_general(
            a, b, (((1,), (contract,)), ((), ())), preferred_element_type=jnp.float32
        )

    def couple(blocks, overs):
        firsts = [dot(o, b, 0).astype(jnp.bfloat16) for o, b in zip(overs, blocks)]
        return [dot(f, o, 1) for f, o in zip(firsts, overs)]

    for sweep in range(ITERS):
        held = (sweep + 1) % 2

        def taken(slot):
            if sweep == 0:
                return amps[slot]
            return current[held, meta[place_at, 0, slot]]

        def send_rows(g):
            for t in range(row_cap):
                row_send[sweep, g * row_cap + t] = taken(want[g, 0, t])
            row_copy(sweep, g).start()

        def send_cols(t):
            for h in range(cols - 1, 0, -1):
                col_send[sweep, h * col_cap + t] = taken(want[rows + h, 0, t])
                col_copy(sweep, h, t).start()

        if sweep == 0:
            for t in range(col_cap):
                send_cols(t)
            take_asked(0, rows, 15).wait()
            for g in range(1, rows):
                send_rows(g)
            moved = place_pairs()
        else:
            row_next = 1
            for t in range(col_cap):
                send_cols(t)
                row_end = 1 + (rows - 1) * (t + 1) // col_cap
                for g in range(row_next, row_end):
                    send_rows(g)
                row_next = row_end
        for t in range(col_cap):
            col_got[sweep, t] = taken(want[rows, 0, t])
        for t in range(row_cap):
            row_got[sweep][t] = taken(want[0, 0, t])

        if sweep == 0:
            moved.wait()
            for load in loads:
                load.wait()

            @pl.loop(0, cols)
            def _(h):
                for t in range(col_cap):
                    p = meta[h, 0, t]
                    occupied = fock[pair_occ[0, p]] + fock[pair_occ[1, p]]
                    across = jnp.broadcast_to(energy[p], (width, width))
                    value = across + across.T - occupied
                    denom[h * col_cap + t] = value
                    inverse[h * col_cap + t] = 1.0 / value
        else:
            wait_sent(sweep - 1)

        for g in range(1, rows):
            row_copy(sweep, g).wait_recv()

        @pl.loop(0, cols)
        def _(h):
            who = [meta[h, 0, t] for t in range(col_cap)]
            overs = [row_over[p] for p in who]
            blocks = [row_got[sweep][meta[from_at, 0, p]] for p in who]
            for t, (p, term) in enumerate(zip(who, couple(blocks, overs))):
                partial[h * col_cap + t] = row_fock[p] * term - ints[p].astype(jnp.float32)

        def col_part(at):
            who = [meta[h, 0, t] for h, t in at]
            overs = [col_over[p] for p in who]
            keys = [h * col_cap + t for h, t in at]
            blocks = [col_got[sweep, k] for k in keys]
            for k, p, term in zip(keys, who, couple(blocks, overs)):
                total = partial[k] + col_fock[p] * term
                if sweep == ITERS - 1:
                    own = current[held, k].astype(jnp.float32)
                    res_sorted[k] = (denom[k] * own - total).astype(jnp.bfloat16)
                current[sweep % 2, k] = (total * inverse[k]).astype(jnp.bfloat16)

        near = min(2, cols)
        for h in range(near):
            if h:
                for t in range(col_cap):
                    col_copy(sweep, h, t).wait_recv()
            col_part([(h, t) for t in range(col_cap)])
        for t in range(col_cap):
            for h in range(near, cols):
                col_copy(sweep, h, t).wait_recv()
            col_part([(h, t) for h in range(near, cols)])

    for p in range(pairs):
        place = meta[place_at, 0, p]
        new_out[p] = current[(ITERS - 1) % 2, place]
        res_out[p] = res_sorted[place]
    wait_sent(ITERS - 1)


def store_kernel(new_in, res_in, new_out, res_out, sem):
    pairs, parts = new_in.shape[0], sem.shape[1]
    copies = []
    for i, (source, target) in enumerate(((new_in, new_out), (res_in, res_out))):
        for part in range(parts):
            first, end = pairs * part // parts, pairs * (part + 1) // parts
            here = pl.ds(first, end - first)
            copies.append(
                pltpu.make_async_copy(source.at[here], target.at[here], sem.at[i, part])
            )
    for copy in copies:
        copy.start()
    for copy in copies:
        copy.wait()


def body(
    amplitudes,
    exchange_ints,
    row_intersection,
    col_intersection,
    pno_energy,
    row_fock,
    col_fock,
    pair_occ,
    fock_occ,
    row_peer,
    row_slot,
    col_peer,
    col_slot,
):
    pairs, width, _ = amplitudes.shape
    rows, cols = lax.axis_size("oj"), lax.axis_size("oi")
    row_cap = max(2, (pairs + rows - 1) // rows + 1)
    col_cap = max(2, (pairs + cols - 1) // cols + 1)
    places = cols * col_cap
    wide = jax.ShapeDtypeStruct(amplitudes.shape, jnp.bfloat16)
    block = (width, width)
    half, full, whole = jnp.bfloat16, jnp.float32, jnp.int32
    vmem, smem = pltpu.VMEM, pltpu.SMEM
    new, res = pl.pallas_call(
        functools.partial(sweep_kernel, rows, cols, row_cap, col_cap),
        out_shape=(vmem(amplitudes.shape, half),) * 2,
        in_specs=[pl.BlockSpec(memory_space=pltpu.HBM)] * 13,
        out_specs=(pl.BlockSpec(memory_space=vmem),) * 2,
        scratch_shapes=[
            vmem((4, 1, pairs), whole),
            vmem((4, 1, LANES), whole),
            vmem((rows + cols, 1, LANES), whole),
            vmem((cols + 2, 1, LANES), whole),
            smem((cols + 2, 1, LANES), whole),
            smem((pairs,), full),
            smem((pairs,), full),
            smem((2, pairs), whole),
            smem(fock_occ.shape, full),
            vmem(amplitudes.shape, half),
            vmem(amplitudes.shape, half),
            vmem(amplitudes.shape, half),
            vmem(amplitudes.shape, half),
            vmem((pairs, 1, width), full),
            vmem((rows + cols, 1, LANES), whole),
            smem((rows + cols, 1, LANES), whole),
            vmem((places,) + block, full),
            vmem((places,) + block, full),
            vmem((places,) + block, full),
            vmem((2, places) + block, half),
            vmem((places,) + block, half),
            vmem((rows * row_cap,) + block, half),
            vmem((rows * row_cap,) + block, half),
            vmem((rows * row_cap,) + block, half),
            vmem((ITERS, places) + block, half),
            vmem((ITERS, rows * row_cap) + block, half),
            vmem((ITERS, places) + block, half),
            pltpu.SemaphoreType.DMA((16,)),
            pltpu.SemaphoreType.DMA((rows + cols,)),
            pltpu.SemaphoreType.DMA((rows + cols,)),
            pltpu.SemaphoreType.DMA((ITERS, rows)),
            pltpu.SemaphoreType.DMA((ITERS, rows)),
            pltpu.SemaphoreType.DMA((ITERS, places)),
            pltpu.SemaphoreType.DMA((ITERS, places)),
        ],
        compiler_params=pltpu.CompilerParams(
            collective_id=0, has_side_effects=True, vmem_limit_bytes=48 * 1024 * 1024
        ),
        name="sweeps",
    )(
        *(pltpu.with_memory_space_constraint(x, pltpu.HBM) for x in (
        row_peer.reshape(1, pairs),
        row_slot.reshape(1, pairs),
        col_peer.reshape(1, pairs),
        col_slot.reshape(1, pairs),
        amplitudes,
        row_fock,
        col_fock,
        pair_occ.T,
        fock_occ,
        exchange_ints,
        row_intersection,
        col_intersection,
        pno_energy.reshape(pairs, 1, width),
        ))
    )
    return pl.pallas_call(
        store_kernel,
        out_shape=(wide, wide),
        in_specs=[pl.BlockSpec(memory_space=vmem)] * 2,
        out_specs=(pl.BlockSpec(memory_space=pltpu.HBM),) * 2,
        scratch_shapes=[pltpu.SemaphoreType.DMA((2, 4))],
        name="store",
    )(new, res)


def solution(mesh):
    return jax.shard_map(
        body,
        mesh=mesh,
        in_specs=(
            P(("oi", "oj"), None, None),
            P(("oi", "oj"), None, None),
            P(("oi", "oj"), None, None),
            P(("oi", "oj"), None, None),
            P(("oi", "oj"), None),
            P(("oi", "oj")),
            P(("oi", "oj")),
            P(("oi", "oj"), None),
            P(),
            P(("oi", "oj"), None),
            P(("oi", "oj")),
            P(("oi", "oj"), None),
            P(("oi", "oj")),
        ),
        out_specs=(P(("oi", "oj"), None, None), P(("oi", "oj"), None, None)),
        check_vma=False,
    )
```

```python
import functools
import jax
import jax.numpy as jnp
from jax import lax
from jax.experimental import pallas as pl
from jax.experimental.pallas import tpu as pltpu
from jax.sharding import PartitionSpec as P

ITERS = 3
LANES = 128


def flip(me, step):
    out = me
    bit = 1
    while bit <= step:
        if step & bit:
            out = out + bit * (1 - 2 * ((me // bit) % 2))
        bit *= 2
    return out


def grouped(peer, me):
    group = (peer ^ me).astype(jnp.float32)
    along = jnp.broadcast_to(group, (LANES, LANES))
    earlier = lax.broadcasted_iota(jnp.int32, (LANES, LANES), 0) < lax.broadcasted_iota(
        jnp.int32, (LANES, LANES), 1
    )
    same = jnp.where((along.T == along) & earlier, 1.0, 0.0)
    return group, jnp.sum(same, axis=0, keepdims=True)


def bounded(values, count):
    return jnp.minimum(jnp.maximum(values.astype(jnp.int32), 0), count - 1)


def listed(group, before, values, count, cap, pairs):
    tall = -(-count // 8) * 8
    which = lax.broadcasted_iota(jnp.int32, (tall, LANES), 0).astype(jnp.float32)
    lane = lax.broadcasted_iota(jnp.int32, (tall, LANES), 1)
    mine = group == which
    out = jnp.zeros((tall, LANES), jnp.float32)
    for t in range(cap):
        one = jnp.sum(jnp.where(mine & (before == t), values, 0.0), axis=1, keepdims=True)
        out = jnp.where(lane == t, one, out)
    return bounded(out, pairs)


def sweep_kernel(
    rows,
    cols,
    row_cap,
    col_cap,
    row_peer_hbm,
    row_slot_hbm,
    col_peer_hbm,
    col_slot_hbm,
    amps_hbm,
    row_fock_hbm,
    col_fock_hbm,
    pair_occ_hbm,
    fock_hbm,
    ints_hbm,
    row_over_hbm,
    col_over_hbm,
    energy_hbm,
    new_out,
    res_out,
    short,
    long,
    table,
    places_in,
    meta,
    row_fock,
    col_fock,
    pair_occ,
    fock,
    amps,
    ints,
    row_over,
    col_over,
    energy,
    want_in,
    want,
    denom,
    inverse,
    partial,
    current,
    res_sorted,
    row_got_0,
    row_got_1,
    row_got_2,
    col_got,
    row_send,
    col_send,
    local_sem,
    table_send_sem,
    table_recv_sem,
    row_send_sem,
    row_recv_sem,
    col_send_sem,
    col_recv_sem,
):
    row_got = (row_got_0, row_got_1, row_got_2)
    places = cols * col_cap
    pairs = amps.shape[0]
    width = amps.shape[1]
    row_me, col_me = lax.axis_index("oj"), lax.axis_index("oi")
    groups = [g for g in range(rows + cols) if g not in (0, rows)]
    place_at, from_at = cols, cols + 1

    def peer(g):
        if g < rows:
            return {"oj": flip(row_me, g)}
        return {"oi": flip(col_me, g - rows)}

    def local(source, target, i):
        return pltpu.make_async_copy(source, target, local_sem.at[i])

    small = [
        local(source, short.at[i], i)
        for i, source in enumerate((row_peer_hbm, row_slot_hbm, col_peer_hbm, col_slot_hbm))
    ]
    first_load = local(amps_hbm, amps, 4)
    loads = [
        local(source, target, 5 + i)
        for i, (source, target) in enumerate(
            (
                (energy_hbm, energy),
                (row_fock_hbm, row_fock),
                (col_fock_hbm, col_fock),
                (pair_occ_hbm, pair_occ),
                (fock_hbm, fock),
                (row_over_hbm, row_over),
                (col_over_hbm, col_over),
                (ints_hbm, ints),
            )
        )
    ]
    for load in small:
        load.start()
    barrier = pltpu.get_barrier_semaphore()
    for g in groups:
        pl.semaphore_signal(
            barrier, inc=1, device_id=peer(g), device_id_type=pl.DeviceIdType.MESH
        )
    first_load.start()
    for load in loads:
        load.start()
    long[...] = jnp.full(long.shape, 1 << 20, jnp.int32)
    for load in small:
        load.wait()
    for i in range(4):
        long[i, :, 0:pairs] = short[i]
    col_group_of, col_before = grouped(long[2], col_me)
    col_asked = listed(col_group_of, col_before, long[3].astype(jnp.float32), cols, col_cap, pairs)
    for g in range(cols):
        table[rows + g] = col_asked[g : g + 1]

    def ask(g):
        return pltpu.make_async_remote_copy(
            src_ref=table.at[g],
            dst_ref=want_in.at[g],
            send_sem=table_send_sem.at[g],
            recv_sem=table_recv_sem.at[g],
            device_id=peer(g),
            device_id_type=pl.DeviceIdType.MESH,
        )

    pl.semaphore_wait(barrier, len(groups))
    for g in range(rows + 1, rows + cols):
        ask(g).start()
    row_group, row_before = grouped(long[0], row_me)
    row_asked = listed(row_group, row_before, long[1].astype(jnp.float32), rows, row_cap, pairs)
    for g in range(rows):
        table[g] = row_asked[g : g + 1]
    for g in range(1, rows):
        ask(g).start()
    want_in[0] = table[0]
    want_in[rows] = table[rows]
    first_load.wait()

    def take_asked(first, count, i):
        for g in range(first + 1, first + count):
            ask(g).wait()
        here = pl.ds(first, count)
        move = local(want_in.at[here], want.at[here], i)
        move.start()
        return move

    take_asked(rows, cols, 14).wait()

    def place_pairs():
        pair_ids = lax.broadcasted_iota(jnp.int32, (1, LANES), 1).astype(jnp.float32)
        order = listed(col_group_of, col_before, pair_ids, cols, col_cap, pairs)
        for h in range(cols):
            places_in[h] = order[h : h + 1]
        places_in[place_at] = bounded(col_group_of * col_cap + col_before, places)
        places_in[from_at] = bounded(row_group * row_cap + row_before, rows * row_cap)
        move = local(places_in, meta, 13)
        move.start()
        return move

    def row_copy(sweep, g):
        here = pl.ds(g * row_cap, row_cap)
        return pltpu.make_async_remote_copy(
            src_ref=row_send.at[sweep, here],
            dst_ref=row_got[sweep].at[here],
            send_sem=row_send_sem.at[sweep, g],
            recv_sem=row_recv_sem.at[sweep, g],
            device_id=peer(g),
            device_id_type=pl.DeviceIdType.MESH,
        )

    def col_copy(sweep, h, t):
        here = pl.ds(h * col_cap + t, 1)
        return pltpu.make_async_remote_copy(
            src_ref=col_send.at[sweep, here],
            dst_ref=col_got.at[sweep, here],
            send_sem=col_send_sem.at[sweep, h * col_cap + t],
            recv_sem=col_recv_sem.at[sweep, h * col_cap + t],
            device_id=peer(rows + h),
            device_id_type=pl.DeviceIdType.MESH,
        )

    def wait_sent(sweep):
        for g in range(1, rows):
            row_copy(sweep, g).wait_send()
        for h in range(1, cols):
            for t in range(col_cap):
                col_copy(sweep, h, t).wait_send()

    def dot(a, b, contract):
        return lax.dot_general(
            a, b, (((1,), (contract,)), ((), ())), preferred_element_type=jnp.float32
        )

    def couple(blocks, overs):
        firsts = [dot(o, b, 0).astype(jnp.bfloat16) for o, b in zip(overs, blocks)]
        return [dot(f, o, 1) for f, o in zip(firsts, overs)]

    for sweep in range(ITERS):
        held = (sweep + 1) % 2

        def taken(slot):
            if sweep == 0:
                return amps[slot]
            return current[held, meta[place_at, 0, slot]]

        def send_rows(g):
            for t in range(row_cap):
                row_send[sweep, g * row_cap + t] = taken(want[g, 0, t])
            row_copy(sweep, g).start()

        def send_cols(t):
            for h in range(cols - 1, 0, -1):
                col_send[sweep, h * col_cap + t] = taken(want[rows + h, 0, t])
                col_copy(sweep, h, t).start()

        if sweep == 0:
            for t in range(col_cap):
                send_cols(t)
            take_asked(0, rows, 15).wait()
            for g in range(1, rows):
                send_rows(g)
            moved = place_pairs()
        else:
            row_next = 1
            for t in range(col_cap):
                send_cols(t)
                row_end = 1 + (rows - 1) * (t + 1) // col_cap
                for g in range(row_next, row_end):
                    send_rows(g)
                row_next = row_end
        for t in range(col_cap):
            col_got[sweep, t] = taken(want[rows, 0, t])
        for t in range(row_cap):
            row_got[sweep][t] = taken(want[0, 0, t])

        if sweep == 0:
            moved.wait()
            for load in loads:
                load.wait()

            @pl.loop(0, cols)
            def _(h):
                for t in range(col_cap):
                    p = meta[h, 0, t]
                    occupied = fock[pair_occ[0, p]] + fock[pair_occ[1, p]]
                    across = jnp.broadcast_to(energy[p], (width, width))
                    value = across + across.T - occupied
                    denom[h * col_cap + t] = value
                    inverse[h * col_cap + t] = 1.0 / value
        else:
            wait_sent(sweep - 1)

        for g in range(1, rows):
            row_copy(sweep, g).wait_recv()

        @pl.loop(0, cols)
        def _(h):
            who = [meta[h, 0, t] for t in range(col_cap)]
            overs = [row_over[p] for p in who]
            blocks = [row_got[sweep][meta[from_at, 0, p]] for p in who]
            for t, (p, term) in enumerate(zip(who, couple(blocks, overs))):
                partial[h * col_cap + t] = row_fock[p] * term - ints[p].astype(jnp.float32)

        def col_part(at):
            who = [meta[h, 0, t] for h, t in at]
            overs = [col_over[p] for p in who]
            keys = [h * col_cap + t for h, t in at]
            blocks = [col_got[sweep, k] for k in keys]
            for k, p, term in zip(keys, who, couple(blocks, overs)):
                total = partial[k] + col_fock[p] * term
                if sweep == ITERS - 1:
                    own = current[held, k].astype(jnp.float32)
                    res_sorted[k] = (denom[k] * own - total).astype(jnp.bfloat16)
                current[sweep % 2, k] = (total * inverse[k]).astype(jnp.bfloat16)

        near = min(2, cols)
        for h in range(near):
            if h:
                for t in range(col_cap):
                    col_copy(sweep, h, t).wait_recv()
            col_part([(h, t) for t in range(col_cap)])
        for t in range(col_cap):
            for h in range(near, cols):
                col_copy(sweep, h, t).wait_recv()
            col_part([(h, t) for h in range(near, cols)])

    for p in range(pairs):
        place = meta[place_at, 0, p]
        new_out[p] = current[(ITERS - 1) % 2, place]
        res_out[p] = res_sorted[place]
    wait_sent(ITERS - 1)


def store_kernel(new_in, res_in, new_out, res_out, sem):
    pairs, parts = new_in.shape[0], sem.shape[1]
    copies = []
    for i, (source, target) in enumerate(((new_in, new_out), (res_in, res_out))):
        for part in range(parts):
            first, end = pairs * part // parts, pairs * (part + 1) // parts
            here = pl.ds(first, end - first)
            copies.append(
                pltpu.make_async_copy(source.at[here], target.at[here], sem.at[i, part])
            )
    for copy in copies:
        copy.start()
    for copy in copies:
        copy.wait()


def body(
    amplitudes,
    exchange_ints,
    row_intersection,
    col_intersection,
    pno_energy,
    row_fock,
    col_fock,
    pair_occ,
    fock_occ,
    row_peer,
    row_slot,
    col_peer,
    col_slot,
):
    pairs, width, _ = amplitudes.shape
    rows, cols = lax.axis_size("oj"), lax.axis_size("oi")
    row_cap = max(2, (pairs + rows - 1) // rows + 1)
    col_cap = max(2, (pairs + cols - 1) // cols + 1)
    places = cols * col_cap
    wide = jax.ShapeDtypeStruct(amplitudes.shape, jnp.bfloat16)
    block = (width, width)
    half, full, whole = jnp.bfloat16, jnp.float32, jnp.int32
    vmem, smem = pltpu.VMEM, pltpu.SMEM
    new, res = pl.pallas_call(
        functools.partial(sweep_kernel, rows, cols, row_cap, col_cap),
        out_shape=(vmem(amplitudes.shape, half),) * 2,
        in_specs=[pl.BlockSpec(memory_space=pltpu.HBM)] * 13,
        out_specs=(pl.BlockSpec(memory_space=vmem),) * 2,
        scratch_shapes=[
            vmem((4, 1, pairs), whole),
            vmem((4, 1, LANES), whole),
            vmem((rows + cols, 1, LANES), whole),
            vmem((cols + 2, 1, LANES), whole),
            smem((cols + 2, 1, LANES), whole),
            smem((pairs,), full),
            smem((pairs,), full),
            smem((2, pairs), whole),
            smem(fock_occ.shape, full),
            vmem(amplitudes.shape, half),
            vmem(amplitudes.shape, half),
            vmem(amplitudes.shape, half),
            vmem(amplitudes.shape, half),
            vmem((pairs, 1, width), full),
            vmem((rows + cols, 1, LANES), whole),
            smem((rows + cols, 1, LANES), whole),
            vmem((places,) + block, full),
            vmem((places,) + block, full),
            vmem((places,) + block, full),
            vmem((2, places) + block, half),
            vmem((places,) + block, half),
            vmem((rows * row_cap,) + block, half),
            vmem((rows * row_cap,) + block, half),
            vmem((rows * row_cap,) + block, half),
            vmem((ITERS, places) + block, half),
            vmem((ITERS, rows * row_cap) + block, half),
            vmem((ITERS, places) + block, half),
            pltpu.SemaphoreType.DMA((16,)),
            pltpu.SemaphoreType.DMA((rows + cols,)),
            pltpu.SemaphoreType.DMA((rows + cols,)),
            pltpu.SemaphoreType.DMA((ITERS, rows)),
            pltpu.SemaphoreType.DMA((ITERS, rows)),
            pltpu.SemaphoreType.DMA((ITERS, places)),
            pltpu.SemaphoreType.DMA((ITERS, places)),
        ],
        compiler_params=pltpu.CompilerParams(
            collective_id=0, has_side_effects=True, vmem_limit_bytes=48 * 1024 * 1024
        ),
        name="sweeps",
    )(
        *(pltpu.with_memory_space_constraint(x, pltpu.HBM) for x in (
        row_peer.reshape(1, pairs),
        row_slot.reshape(1, pairs),
        col_peer.reshape(1, pairs),
        col_slot.reshape(1, pairs),
        amplitudes,
        row_fock,
        col_fock,
        pair_occ.T,
        fock_occ,
        exchange_ints,
        row_intersection,
        col_intersection,
        pno_energy.reshape(pairs, 1, width),
        ))
    )
    return pl.pallas_call(
        store_kernel,
        out_shape=(wide, wide),
        in_specs=[pl.BlockSpec(memory_space=vmem)] * 2,
        out_specs=(pl.BlockSpec(memory_space=pltpu.HBM),) * 2,
        scratch_shapes=[pltpu.SemaphoreType.DMA((2, 4))],
        compiler_params=pltpu.CompilerParams(vmem_limit_bytes=1024 * 1024),
        name="store",
    )(new, res)


def solution(mesh):
    return jax.shard_map(
        body,
        mesh=mesh,
        in_specs=(
            P(("oi", "oj"), None, None),
            P(("oi", "oj"), None, None),
            P(("oi", "oj"), None, None),
            P(("oi", "oj"), None, None),
            P(("oi", "oj"), None),
            P(("oi", "oj")),
            P(("oi", "oj")),
            P(("oi", "oj"), None),
            P(),
            P(("oi", "oj"), None),
            P(("oi", "oj")),
            P(("oi", "oj"), None),
            P(("oi", "oj")),
        ),
        out_specs=(P(("oi", "oj"), None, None), P(("oi", "oj"), None, None)),
        check_vma=False,
    )
```

```python
import functools
import jax
import jax.numpy as jnp
from jax import lax
from jax.experimental import pallas as pl
from jax.experimental.pallas import tpu as pltpu
from jax.sharding import PartitionSpec as P

ITERS = 3
LANES = 128


def flip(me, step):
    out = me
    bit = 1
    while bit <= step:
        if step & bit:
            out = out + bit * (1 - 2 * ((me // bit) % 2))
        bit *= 2
    return out


def grouped(peer, me):
    group = (peer ^ me).astype(jnp.float32)
    along = jnp.broadcast_to(group, (LANES, LANES))
    earlier = lax.broadcasted_iota(jnp.int32, (LANES, LANES), 0) < lax.broadcasted_iota(
        jnp.int32, (LANES, LANES), 1
    )
    same = jnp.where((along.T == along) & earlier, 1.0, 0.0)
    return group, jnp.sum(same, axis=0, keepdims=True)


def bounded(values, count):
    return jnp.minimum(jnp.maximum(values.astype(jnp.int32), 0), count - 1)


def listed(group, before, values, count, cap, pairs):
    tall = -(-count // 8) * 8
    which = lax.broadcasted_iota(jnp.int32, (tall, LANES), 0).astype(jnp.float32)
    lane = lax.broadcasted_iota(jnp.int32, (tall, LANES), 1)
    mine = group == which
    out = jnp.zeros((tall, LANES), jnp.float32)
    for t in range(cap):
        one = jnp.sum(jnp.where(mine & (before == t), values, 0.0), axis=1, keepdims=True)
        out = jnp.where(lane == t, one, out)
    return bounded(out, pairs)


def sweep_kernel(
    rows,
    cols,
    row_cap,
    col_cap,
    row_peer_hbm,
    row_slot_hbm,
    col_peer_hbm,
    col_slot_hbm,
    amps_hbm,
    row_fock_hbm,
    col_fock_hbm,
    pair_occ_hbm,
    fock_hbm,
    ints_hbm,
    row_over_hbm,
    col_over_hbm,
    energy_hbm,
    new_out,
    res_out,
    short,
    long,
    table,
    places_in,
    meta,
    row_fock,
    col_fock,
    pair_occ,
    fock,
    amps,
    ints,
    row_over,
    col_over,
    energy,
    want_in,
    want,
    denom,
    inverse,
    partial,
    current,
    res_sorted,
    row_got_0,
    row_got_1,
    row_got_2,
    col_got,
    row_send,
    col_send,
    local_sem,
    table_send_sem,
    table_recv_sem,
    row_send_sem,
    row_recv_sem,
    col_send_sem,
    col_recv_sem,
):
    row_got = (row_got_0, row_got_1, row_got_2)
    places = cols * col_cap
    pairs = amps.shape[0]
    width = amps.shape[1]
    row_me, col_me = lax.axis_index("oj"), lax.axis_index("oi")
    groups = [g for g in range(rows + cols) if g not in (0, rows)]
    place_at, from_at = cols, cols + 1

    def peer(g):
        if g < rows:
            return {"oj": flip(row_me, g)}
        return {"oi": flip(col_me, g - rows)}

    def local(source, target, i):
        return pltpu.make_async_copy(source, target, local_sem.at[i])

    small = [
        local(source, short.at[i], i)
        for i, source in enumerate((row_peer_hbm, row_slot_hbm, col_peer_hbm, col_slot_hbm))
    ]
    first_load = local(amps_hbm, amps, 4)
    loads = [
        local(source, target, 5 + i)
        for i, (source, target) in enumerate(
            (
                (energy_hbm, energy),
                (row_fock_hbm, row_fock),
                (col_fock_hbm, col_fock),
                (pair_occ_hbm, pair_occ),
                (fock_hbm, fock),
                (row_over_hbm, row_over),
                (col_over_hbm, col_over),
                (ints_hbm, ints),
            )
        )
    ]
    for load in small:
        load.start()
    barrier = pltpu.get_barrier_semaphore()
    for g in groups:
        pl.semaphore_signal(
            barrier, inc=1, device_id=peer(g), device_id_type=pl.DeviceIdType.MESH
        )
    first_load.start()
    for load in loads:
        load.start()
    long[...] = jnp.full(long.shape, 1 << 20, jnp.int32)
    for load in small:
        load.wait()
    for i in range(4):
        long[i, :, 0:pairs] = short[i]
    col_group_of, col_before = grouped(long[2], col_me)
    col_asked = listed(col_group_of, col_before, long[3].astype(jnp.float32), cols, col_cap, pairs)
    for g in range(cols):
        table[rows + g] = col_asked[g : g + 1]

    def ask(g):
        return pltpu.make_async_remote_copy(
            src_ref=table.at[g],
            dst_ref=want_in.at[g],
            send_sem=table_send_sem.at[g],
            recv_sem=table_recv_sem.at[g],
            device_id=peer(g),
            device_id_type=pl.DeviceIdType.MESH,
        )

    pl.semaphore_wait(barrier, len(groups))
    for g in range(rows + 1, rows + cols):
        ask(g).start()
    row_group, row_before = grouped(long[0], row_me)
    row_asked = listed(row_group, row_before, long[1].astype(jnp.float32), rows, row_cap, pairs)
    for g in range(rows):
        table[g] = row_asked[g : g + 1]
    for g in range(1, rows):
        ask(g).start()
    want_in[0] = table[0]
    want_in[rows] = table[rows]
    first_load.wait()

    def take_asked(first, count, i):
        for g in range(first + 1, first + count):
            ask(g).wait()
        here = pl.ds(first, count)
        move = local(want_in.at[here], want.at[here], i)
        move.start()
        return move

    take_asked(rows, cols, 14).wait()

    def place_pairs():
        pair_ids = lax.broadcasted_iota(jnp.int32, (1, LANES), 1).astype(jnp.float32)
        order = listed(col_group_of, col_before, pair_ids, cols, col_cap, pairs)
        for h in range(cols):
            places_in[h] = order[h : h + 1]
        places_in[place_at] = bounded(col_group_of * col_cap + col_before, places)
        places_in[from_at] = bounded(row_group * row_cap + row_before, rows * row_cap)
        move = local(places_in, meta, 13)
        move.start()
        return move

    def row_copy(sweep, g):
        here = pl.ds(g * row_cap, row_cap)
        return pltpu.make_async_remote_copy(
            src_ref=row_send.at[sweep, here],
            dst_ref=row_got[sweep].at[here],
            send_sem=row_send_sem.at[sweep, g],
            recv_sem=row_recv_sem.at[sweep, g],
            device_id=peer(g),
            device_id_type=pl.DeviceIdType.MESH,
        )

    def col_copy(sweep, h, t):
        here = pl.ds(h * col_cap + t, 1)
        return pltpu.make_async_remote_copy(
            src_ref=col_send.at[sweep, here],
            dst_ref=col_got.at[sweep, here],
            send_sem=col_send_sem.at[sweep, h * col_cap + t],
            recv_sem=col_recv_sem.at[sweep, h * col_cap + t],
            device_id=peer(rows + h),
            device_id_type=pl.DeviceIdType.MESH,
        )

    near = min(2, cols)

    def wait_sent(sweep, far=True):
        for g in range(1, rows):
            row_copy(sweep, g).wait_send()
        for h in range(1, cols if far else near):
            for t in range(col_cap):
                col_copy(sweep, h, t).wait_send()

    def dot(a, b, contract):
        return lax.dot_general(
            a, b, (((1,), (contract,)), ((), ())), preferred_element_type=jnp.float32
        )

    def couple(blocks, overs):
        firsts = [dot(o, b, 0).astype(jnp.bfloat16) for o, b in zip(overs, blocks)]
        return [dot(f, o, 1) for f, o in zip(firsts, overs)]

    for sweep in range(ITERS):
        held = (sweep + 1) % 2

        def taken(slot):
            if sweep == 0:
                return amps[slot]
            return current[held, meta[place_at, 0, slot]]

        def send_rows(g):
            for t in range(row_cap):
                row_send[sweep, g * row_cap + t] = taken(want[g, 0, t])
            row_copy(sweep, g).start()

        def send_cols(t):
            for h in range(cols - 1, 0, -1):
                col_send[sweep, h * col_cap + t] = taken(want[rows + h, 0, t])
                col_copy(sweep, h, t).start()

        for t in range(col_cap):
            send_cols(t)
        if sweep == 0:
            take_asked(0, rows, 15).wait()
        for g in range(1, rows):
            send_rows(g)
        if sweep == 0:
            moved = place_pairs()
        for t in range(col_cap):
            col_got[sweep, t] = taken(want[rows, 0, t])
        for t in range(row_cap):
            row_got[sweep][t] = taken(want[0, 0, t])

        if sweep == 0:
            moved.wait()
            for load in loads:
                load.wait()

            @pl.loop(0, cols)
            def _(h):
                for t in range(col_cap):
                    p = meta[h, 0, t]
                    occupied = fock[pair_occ[0, p]] + fock[pair_occ[1, p]]
                    across = jnp.broadcast_to(energy[p], (width, width))
                    value = across + across.T - occupied
                    denom[h * col_cap + t] = value
                    inverse[h * col_cap + t] = 1.0 / value
        else:
            wait_sent(sweep - 1)

        for g in range(1, rows):
            row_copy(sweep, g).wait_recv()

        @pl.loop(0, cols)
        def _(h):
            who = [meta[h, 0, t] for t in range(col_cap)]
            overs = [row_over[p] for p in who]
            blocks = [row_got[sweep][meta[from_at, 0, p]] for p in who]
            for t, (p, term) in enumerate(zip(who, couple(blocks, overs))):
                partial[h * col_cap + t] = row_fock[p] * term - ints[p].astype(jnp.float32)

        def col_part(at):
            who = [meta[h, 0, t] for h, t in at]
            overs = [col_over[p] for p in who]
            keys = [h * col_cap + t for h, t in at]
            blocks = [col_got[sweep, k] for k in keys]
            for k, p, term in zip(keys, who, couple(blocks, overs)):
                total = partial[k] + col_fock[p] * term
                if sweep == ITERS - 1:
                    own = current[held, k].astype(jnp.float32)
                    res_sorted[k] = (denom[k] * own - total).astype(jnp.bfloat16)
                current[sweep % 2, k] = (total * inverse[k]).astype(jnp.bfloat16)

        for h in range(near):
            if h:
                for t in range(col_cap):
                    col_copy(sweep, h, t).wait_recv()
            col_part([(h, t) for t in range(col_cap)])
        if sweep == ITERS - 1:
            wait_sent(sweep, far=False)
        for t in range(col_cap):
            for h in range(near, cols):
                col_copy(sweep, h, t).wait_recv()
            col_part([(h, t) for h in range(near, cols)])

    for p in range(pairs):
        place = meta[place_at, 0, p]
        new_out[p] = current[(ITERS - 1) % 2, place]
        res_out[p] = res_sorted[place]
    for h in range(near, cols):
        for t in range(col_cap):
            col_copy(ITERS - 1, h, t).wait_send()


def store_kernel(new_in, res_in, new_out, res_out, sem):
    pairs, parts = new_in.shape[0], sem.shape[1]
    copies = []
    for i, (source, target) in enumerate(((new_in, new_out), (res_in, res_out))):
        for part in range(parts):
            first, end = pairs * part // parts, pairs * (part + 1) // parts
            here = pl.ds(first, end - first)
            copies.append(
                pltpu.make_async_copy(source.at[here], target.at[here], sem.at[i, part])
            )
    for copy in copies:
        copy.start()
    for copy in copies:
        copy.wait()


def body(
    amplitudes,
    exchange_ints,
    row_intersection,
    col_intersection,
    pno_energy,
    row_fock,
    col_fock,
    pair_occ,
    fock_occ,
    row_peer,
    row_slot,
    col_peer,
    col_slot,
):
    pairs, width, _ = amplitudes.shape
    rows, cols = lax.axis_size("oj"), lax.axis_size("oi")
    row_cap = max(2, (pairs + rows - 1) // rows + 1)
    col_cap = max(2, (pairs + cols - 1) // cols + 1)
    places = cols * col_cap
    wide = jax.ShapeDtypeStruct(amplitudes.shape, jnp.bfloat16)
    block = (width, width)
    half, full, whole = jnp.bfloat16, jnp.float32, jnp.int32
    vmem, smem = pltpu.VMEM, pltpu.SMEM
    new, res = pl.pallas_call(
        functools.partial(sweep_kernel, rows, cols, row_cap, col_cap),
        out_shape=(vmem(amplitudes.shape, half),) * 2,
        in_specs=[pl.BlockSpec(memory_space=pltpu.HBM)] * 13,
        out_specs=(pl.BlockSpec(memory_space=vmem),) * 2,
        scratch_shapes=[
            vmem((4, 1, pairs), whole),
            vmem((4, 1, LANES), whole),
            vmem((rows + cols, 1, LANES), whole),
            vmem((cols + 2, 1, LANES), whole),
            smem((cols + 2, 1, LANES), whole),
            smem((pairs,), full),
            smem((pairs,), full),
            smem((2, pairs), whole),
            smem(fock_occ.shape, full),
            vmem(amplitudes.shape, half),
            vmem(amplitudes.shape, half),
            vmem(amplitudes.shape, half),
            vmem(amplitudes.shape, half),
            vmem((pairs, 1, width), full),
            vmem((rows + cols, 1, LANES), whole),
            smem((rows + cols, 1, LANES), whole),
            vmem((places,) + block, full),
            vmem((places,) + block, full),
            vmem((places,) + block, full),
            vmem((2, places) + block, half),
            vmem((places,) + block, half),
            vmem((rows * row_cap,) + block, half),
            vmem((rows * row_cap,) + block, half),
            vmem((rows * row_cap,) + block, half),
            vmem((ITERS, places) + block, half),
            vmem((ITERS, rows * row_cap) + block, half),
            vmem((ITERS, places) + block, half),
            pltpu.SemaphoreType.DMA((16,)),
            pltpu.SemaphoreType.DMA((rows + cols,)),
            pltpu.SemaphoreType.DMA((rows + cols,)),
            pltpu.SemaphoreType.DMA((ITERS, rows)),
            pltpu.SemaphoreType.DMA((ITERS, rows)),
            pltpu.SemaphoreType.DMA((ITERS, places)),
            pltpu.SemaphoreType.DMA((ITERS, places)),
        ],
        compiler_params=pltpu.CompilerParams(
            collective_id=0, has_side_effects=True, vmem_limit_bytes=48 * 1024 * 1024
        ),
        name="sweeps",
    )(
        *(pltpu.with_memory_space_constraint(x, pltpu.HBM) for x in (
        row_peer.reshape(1, pairs),
        row_slot.reshape(1, pairs),
        col_peer.reshape(1, pairs),
        col_slot.reshape(1, pairs),
        amplitudes,
        row_fock,
        col_fock,
        pair_occ.T,
        fock_occ,
        exchange_ints,
        row_intersection,
        col_intersection,
        pno_energy.reshape(pairs, 1, width),
        ))
    )
    return pl.pallas_call(
        store_kernel,
        out_shape=(wide, wide),
        in_specs=[pl.BlockSpec(memory_space=vmem)] * 2,
        out_specs=(pl.BlockSpec(memory_space=pltpu.HBM),) * 2,
        scratch_shapes=[pltpu.SemaphoreType.DMA((2, 4))],
        compiler_params=pltpu.CompilerParams(vmem_limit_bytes=1024 * 1024),
        name="store",
    )(new, res)


def solution(mesh):
    return jax.shard_map(
        body,
        mesh=mesh,
        in_specs=(
            P(("oi", "oj"), None, None),
            P(("oi", "oj"), None, None),
            P(("oi", "oj"), None, None),
            P(("oi", "oj"), None, None),
            P(("oi", "oj"), None),
            P(("oi", "oj")),
            P(("oi", "oj")),
            P(("oi", "oj"), None),
            P(),
            P(("oi", "oj"), None),
            P(("oi", "oj")),
            P(("oi", "oj"), None),
            P(("oi", "oj")),
        ),
        out_specs=(P(("oi", "oj"), None, None), P(("oi", "oj"), None, None)),
        check_vma=False,
    )
```
